32 devices in a mesh: dst: 8 (over y, x, core), src: 4 (over z).
Axes of the slice: x: 2, y: 2, z: 4, core: 2. Of those that a mesh axis runs over, the one named last changes fastest.
Arguments:
- points: bfloat16 [4096, 256], P(('dst', 'src')), may hold values from -6 to 6
- w_query: bfloat16 [256, 256], replicated, may hold values from -16 to 16
- w_key: bfloat16 [256, 256], replicated, may hold values from -0.375 to 0.375
- w_value: bfloat16 [256, 256], replicated, may hold values from -0.375 to 0.375
- w_out: bfloat16 [256, 256], replicated, may hold values from -0.375 to 0.375
- gain: float32 [256], replicated, may hold values from 0.25 to 1.75
- cell_counts: int32 [8, 4], P('dst', 'src'), may hold values from 2 to 16, as said below
- tile_slots: int32 [8, 4, 16], P('dst', 'src'), may hold values from 0 to 31, as said below
- edge_masks: int32 [8, 4, 16, 128, 128], P('dst', 'src'), may hold values 0 or 1
Outputs:
- out_points: bfloat16 [4096, 256], P(('dst', 'src'))
The draws below stay inside these ranges and needn't reach their ends.
Inputs may be any that keep to these rules, and one draw needn't show every extreme that they name: `cell_counts`: the busiest cell lists exactly 16 tiles. `tile_slots`: within one cell the 16 tile numbers are all different.
All inputs are finite; a program needn't handle non-finite values. No bound on the sum of `edge_masks` on one device may be relied on, other than what follows from the above.
Results may differ from the reference program's by a relative error of at most 0.0085.
The reference program's roundings to bfloat16 on the way (of `tangent`, `queries` and `mixed`) count: a program that leaves them out, or rounds other values in their place, can miss the bound.
Values may be sent and summed in bfloat16 or wider, within the bound.
A program may use at most 64 MiB of HBM per device.

```python
import math
import jax
import jax.numpy as jnp
from jax import lax

D = 256
HEADS = 4
TILE = 128
NODE_DEV = 128
NODES = 4096
TILES = 16
N_DST = 8
N_SRC = 4


def draw_w_query(key, part):
    base = jax.random.normal(key, (D, D), jnp.float32) * D ** (-0.5)
    return base.astype(jnp.bfloat16)


def draw_cell_counts(key, part):
    least_count = max(1, TILES // 8)
    counts = jax.random.randint(key, (N_DST * N_SRC,), least_count, TILES + 1, dtype=jnp.int32)
    busiest = jax.random.randint(jax.random.fold_in(key, 3), (), 0, N_DST * N_SRC, dtype=jnp.int32)
    counts = counts.at[busiest].set(TILES)
    return counts.reshape(N_DST, N_SRC)


def draw_tile_slots(key, part):
    grid_tiles = N_SRC * NODE_DEV // TILE * (N_DST * NODE_DEV // TILE)
    cell_keys = jax.random.split(key, N_DST * N_SRC)

    def one_cell(cell_key):
        return jax.random.permutation(cell_key, grid_tiles)[:TILES].astype(jnp.int32)
    return jax.vmap(one_cell)(cell_keys).reshape(N_DST, N_SRC, TILES)


def place_ends(drawn, stream_key, least, top_value):
    shape = drawn.shape
    index_at = [jax.random.randint(jax.random.fold_in(stream_key, axis), (), 0, shape[axis]) for axis in range(len(shape))]
    drawn = drawn.at[tuple(index_at)].set(least)
    longest = shape.index(max(shape))
    index_at[longest] = (index_at[longest] + 1) % shape[longest]
    return drawn.at[tuple(index_at)].set(top_value)


def block_levels(key, extent, cuts, least, top_value):
    def one(dim, blocks):
        heights = jax.random.uniform(jax.random.fold_in(jax.random.fold_in(key, 6), dim), (blocks,), jnp.float32, least / len(cuts), top_value / len(cuts))
        return jnp.repeat(jnp.exp(heights), extent[dim] // blocks).reshape((-1,) + (1,) * (len(extent) - dim - 1))

    level = one(*cuts[0])
    for cut in cuts[1:]:
        level = level * one(*cut)
    return level


def scatter_about(rng, dims, spread, most, pieces=(), held_as=jnp.bfloat16):
    values = jax.random.normal(rng, dims, jnp.float32) * spread
    if len(pieces) > 0:
        values = block_levels(rng, dims, pieces, -0.22, 0.18) * values
    return jnp.clip(values, min=-most, max=most).astype(held_as)


def setup_inputs(seed: int = 0) -> dict:
    streams_of = jax.random.split(jax.random.key(seed), 10)
    return {
        "points": scatter_about(streams_of[0], (NODES, D), 1.0, 6.0, ((0, 32),)),
        "w_query": draw_w_query(jax.random.fold_in(streams_of[9], 71), 0),
        "w_key": scatter_about(streams_of[2], (D, D), D ** -0.5, 0.375),
        "w_value": scatter_about(streams_of[3], (D, D), D ** -0.5, 0.375),
        "w_out": scatter_about(streams_of[4], (D, D), D ** -0.5, 0.375),
        "gain": jnp.clip(1.0 + 0.15 * jax.random.normal(streams_of[5], (D,), jnp.float32), 0.25, 1.75),
        "cell_counts": draw_cell_counts(jax.random.fold_in(streams_of[9], 71), 0),
        "tile_slots": draw_tile_slots(jax.random.fold_in(streams_of[9], 71), 0),
        "edge_masks": place_ends((jax.random.randint(streams_of[8], (N_DST, N_SRC, TILES, TILE, TILE), 0, 64) < 1).astype(jnp.int32), jax.random.fold_in(streams_of[8], 1), 0, 1),
    }


def inverse_sinh(ratio):
    return jnp.log(ratio + jnp.sqrt(ratio * ratio + 1.0))

def log_map(points):
    values_f = points.astype(jnp.float32)
    radius = jnp.sqrt(lax.optimization_barrier(jnp.sum(values_f * values_f, axis=-1, keepdims=True)) + 1e-06)
    root_width = math.sqrt(points.shape[-1])
    return (root_width * inverse_sinh(radius / root_width) * values_f / radius).astype(jnp.bfloat16)

def exp_map(normed):
    radius = jnp.sqrt(lax.optimization_barrier(jnp.sum(normed * normed, axis=-1, keepdims=True)) + 1e-06)
    root_width = math.sqrt(normed.shape[-1])
    return (root_width * jnp.sinh(radius / root_width) * normed / radius).astype(jnp.bfloat16)

def project(rows, weight):
    return jnp.dot(rows, weight, preferred_element_type=jnp.float32).astype(jnp.bfloat16)

def reference(points, w_query, w_key, w_value, w_out, gain, cell_counts, tile_slots, edge_masks):
    head_size = D // HEADS
    score_scale = 1.0 / math.sqrt(head_size)
    tangent = log_map(points)
    queries = project(tangent, w_query)
    keys = project(tangent, w_key)
    values = project(tangent, w_value)
    block_rows = N_SRC * NODE_DEV
    row_tiles = block_rows // TILE
    col_tiles = N_DST * NODE_DEV // TILE
    key_src = keys.reshape(N_DST, N_SRC, NODE_DEV, D).transpose(1, 0, 2, 3).reshape(N_SRC, col_tiles, TILE, HEADS, head_size)
    value_src = values.reshape(N_DST, N_SRC, NODE_DEV, D).transpose(1, 0, 2, 3).reshape(N_SRC, col_tiles, TILE, HEADS, head_size)
    query_blocks = queries.reshape(N_DST, row_tiles, TILE, HEADS, head_size)
    key_blocks = keys.reshape(N_DST, block_rows, HEADS, head_size)
    value_blocks = values.reshape(N_DST, block_rows, HEADS, head_size)
    live_slots = jnp.arange(TILES, dtype=jnp.int32)[None, None, :] < cell_counts[:, :, None]
    src_ids = jnp.arange(N_SRC, dtype=jnp.int32)[:, None]
    inner_rows = jnp.arange(TILE, dtype=jnp.int32)

    def one_block(inputs):
        q_block, k_block, v_block, slot_grid, mask_grid, live_grid = inputs
        row_ids = (slot_grid // col_tiles).astype(jnp.int32)
        col_ids = (slot_grid % col_tiles).astype(jnp.int32)
        q_tiles = q_block[row_ids].astype(jnp.float32)
        k_tiles = key_src[src_ids, col_ids].astype(jnp.float32)
        v_tiles = value_src[src_ids, col_ids].astype(jnp.float32)
        scores = jnp.einsum('stihe,stjhe->sthij', q_tiles, k_tiles, precision=lax.Precision.HIGHEST) * score_scale
        edge_live = ((mask_grid == 1) & live_grid[:, :, None, None])[:, :, None]
        tile_max = lax.optimization_barrier(jnp.max(jnp.where(edge_live, scores, -jnp.inf), axis=-1))
        q_rows = q_block.reshape(block_rows, HEADS, head_size).astype(jnp.float32)
        self_score = jnp.einsum('rhe,rhe->hr', q_rows, k_block.astype(jnp.float32), precision=lax.Precision.HIGHEST) * score_scale
        flat_rows = (row_ids[:, :, None] * TILE + inner_rows[None, None, :]).reshape(-1)
        row_max = self_score.at[:, flat_rows].max(tile_max.transpose(2, 0, 1, 3).reshape(HEADS, -1))
        gathered_max = row_max[:, flat_rows].reshape(HEADS, N_SRC, TILES, TILE).transpose(1, 2, 0, 3)
        weights = jnp.where(edge_live, jnp.exp(scores - gathered_max[..., None]), 0.0)
        tile_sum = lax.optimization_barrier(jnp.sum(weights, axis=-1))
        self_exp = jnp.exp(self_score - row_max)
        row_sum = self_exp.at[:, flat_rows].add(tile_sum.transpose(2, 0, 1, 3).reshape(HEADS, -1))
        weights_low = lax.optimization_barrier(weights.astype(jnp.bfloat16)).astype(jnp.float32)
        tile_acc = jnp.einsum('sthij,stjhe->stihe', weights_low, v_tiles, precision=lax.Precision.HIGHEST)
        self_weight = lax.optimization_barrier(self_exp.astype(jnp.bfloat16)).astype(jnp.float32)
        row_acc = self_weight.T[:, :, None] * v_block.astype(jnp.float32)
        row_acc = row_acc.at[flat_rows].add(tile_acc.reshape(-1, HEADS, head_size))
        mixed_rows = row_acc / row_sum.T[:, :, None]
        return mixed_rows.reshape(block_rows, D).astype(jnp.bfloat16)
    mixed = lax.map(one_block, (query_blocks, key_blocks, value_blocks, tile_slots, edge_masks, live_slots))
    mixed = mixed.reshape(-1, D)
    shifted = tangent.astype(jnp.float32) + jnp.dot(mixed, w_out, preferred_element_type=jnp.float32)
    normed = shifted / jnp.sqrt(lax.optimization_barrier(jnp.mean(shifted * shifted, axis=-1, keepdims=True)) + 1e-06) * gain
    return exp_map(normed)
```

```python
import functools
import math

import jax
import jax.numpy as jnp
from jax import lax
from jax.experimental import pallas as pl
from jax.experimental.pallas import tpu as pltpu
from jax.sharding import PartitionSpec as P

HEADS = 4
NEG = -1e30
MESH = pl.DeviceIdType.MESH


def dot(a, b, dims=((1,), (0,))):
    return lax.dot_general(a, b, (dims, ((), ())), preferred_element_type=jnp.float32)


def log_map(points):
    values_f = points.astype(jnp.float32)
    radius = jnp.sqrt(jnp.sum(values_f * values_f, axis=-1, keepdims=True) + 1e-06)
    root_width = math.sqrt(points.shape[-1])
    ratio = radius / root_width
    arc = jnp.log(ratio + jnp.sqrt(ratio * ratio + 1.0))
    return (values_f * (root_width * arc / radius)).astype(jnp.bfloat16)


def sinh_over(x):
    sq = x * x
    series = 1.0 + sq / 6.0 * (1.0 + sq / 20.0 * (1.0 + sq / 42.0 * (1.0 + sq / 72.0)))
    grown = jnp.exp(x)
    return jnp.where(x < 1.0, series, 0.5 * (grown - 1.0 / grown) / x)


def fold_rows(x):
    return x.reshape(x.shape[0] // 8, 8, x.shape[1])


def kernel(
    n_dst, n_src, tile, n_slots,
    points_ref, wq_ref, wk_ref, wv_ref, wo_ref, gain_ref, counts_ref, slots_ref, masks_hbm,
    out_ref,
    kt, qt, masks, bias, inv, k_all, v_all, scores, probs, acc_out, stat_out, acc_in, stat_in,
    mask_sem, kt_send, kt_recv, qt_send, qt_recv, acc_send, acc_recv, stat_send, stat_recv,
):
    d = lax.axis_index("dst")
    s = lax.axis_index("src")
    width = points_ref.shape[1]
    head = width // HEADS
    scale = 1.0 / math.sqrt(head)

    def dst_peer(off):
        return lax.rem(d + off, n_dst)

    def src_peer(off):
        return lax.rem(s + off, n_src)

    barrier = pltpu.get_barrier_semaphore()
    for off in range(1, n_src):
        pl.semaphore_signal(barrier, inc=1, device_id=(d, src_peer(off)), device_id_type=MESH)
    for off in range(1, n_dst):
        pl.semaphore_signal(barrier, inc=1, device_id=(dst_peer(off), s), device_id_type=MESH)

    mask_copy = pltpu.make_async_copy(masks_hbm, masks, mask_sem)
    mask_copy.start()
    tangent = log_map(points_ref[...])
    kt[d] = tangent
    qt[s] = tangent
    pl.semaphore_wait(barrier, n_src - 1 + n_dst - 1)

    def q_copy(slot, peer):
        return pltpu.make_async_remote_copy(
            src_ref=qt.at[slot], dst_ref=qt.at[slot],
            send_sem=qt_send.at[peer], recv_sem=qt_recv.at[slot],
            device_id=(d, peer), device_id_type=MESH)

    def k_copy(slot, peer):
        return pltpu.make_async_remote_copy(
            src_ref=kt.at[slot], dst_ref=kt.at[slot],
            send_sem=kt_send.at[peer], recv_sem=kt_recv.at[slot],
            device_id=(peer, s), device_id_type=MESH)

    src_order = [2, 1, 3] if n_src == 4 else list(range(1, n_src))
    for off in src_order:
        q_copy(s, src_peer(off)).start()
    for off in range(1, n_dst):
        k_copy(d, dst_peer(off)).start()

    own_q = dot(tangent, wq_ref[...]).astype(jnp.bfloat16).astype(jnp.float32).T
    own_k = dot(tangent, wk_ref[...]).astype(jnp.bfloat16).astype(jnp.float32).T
    own_v = dot(tangent, wv_ref[...]).T.astype(jnp.bfloat16).astype(jnp.float32)
    self_score = [
        jnp.sum((own_q * own_k)[h * head:(h + 1) * head], axis=0, keepdims=True) * scale
        for h in range(HEADS)
    ]

    count = counts_ref[0]

    def find_slot(index, carry):
        found = jnp.int32(n_slots)
        for t in range(n_slots):
            found = jnp.where((slots_ref[t] == index) & (count > t), jnp.int32(t), found)
        inv[index] = found
        return carry

    lax.fori_loop(0, n_src * n_dst, find_slot, 0)

    mask_copy.wait()
    bias[n_slots] = jnp.full((tile, tile), NEG, jnp.float32)

    def turn_mask(t, carry):
        bias[t] = jnp.where(masks[t] == 1, 0.0, NEG).astype(jnp.float32).T
        return carry

    lax.fori_loop(0, n_slots, turn_mask, 0)

    def project_slot(slot):
        rows = kt[slot]
        at = pl.ds(pl.multiple_of(slot * tile, tile), tile)
        k_all[at, :] = dot(rows, wk_ref[...]).astype(jnp.bfloat16)
        v_all[:, at] = dot(rows, wv_ref[...]).T.astype(jnp.bfloat16)

    project_slot(d)

    def take_keys(off, carry):
        slot = dst_peer(off)
        k_copy(slot, slot).wait_recv()
        project_slot(slot)
        return carry

    lax.fori_loop(1, n_dst, take_keys, 0)

    group = min(8, n_dst)
    feature_head = lax.broadcasted_iota(jnp.int32, (tile, width), 1) // head

    def over_groups(body, start):
        if n_dst == group:
            return body(0, start)
        return lax.fori_loop(0, n_dst // group, body, start)

    def attend(r):
        q = dot(qt[r], wq_ref[...]).astype(jnp.bfloat16).astype(jnp.float32) * scale
        q_heads = jnp.concatenate(
            [jnp.where(feature_head == h, q, 0.0).astype(jnp.bfloat16) for h in range(HEADS)], axis=0)

        def score_group(g, tops):
            tops = list(tops)
            for member in range(group):
                k = g * group + member
                at = pl.ds(k * tile, tile) if isinstance(k, int) else pl.ds(pl.multiple_of(k * tile, tile), tile)
                prod = dot(k_all[at, :], q_heads, ((1,), (1,)))
                term = bias[inv[r * n_dst + k]]
                for h in range(HEADS):
                    part = prod[:, h * tile:(h + 1) * tile] + term
                    scores[at, h * tile:(h + 1) * tile] = part
                    tops[h] = jnp.maximum(tops[h], jnp.max(fold_rows(part), axis=0))
            return tuple(tops)

        tops = over_groups(score_group, tuple(jnp.full((8, tile), NEG, jnp.float32) for _ in range(HEADS)))
        tops = [jnp.max(t, axis=0, keepdims=True) for t in tops]

        def exp_group(g, sums):
            sums = list(sums)
            for member in range(group):
                k = g * group + member
                at = pl.ds(k * tile, tile) if isinstance(k, int) else pl.ds(pl.multiple_of(k * tile, tile), tile)
                for h in range(HEADS):
                    lanes = slice(h * tile, (h + 1) * tile)
                    p = jnp.exp(scores[at, lanes] - tops[h])
                    sums[h] = sums[h] + jnp.sum(fold_rows(p), axis=0)
                    probs[at, lanes] = p.astype(jnp.bfloat16)
            return tuple(sums)

        sums = over_groups(exp_group, tuple(jnp.zeros((8, tile), jnp.float32) for _ in range(HEADS)))
        sums = [jnp.sum(t, axis=0, keepdims=True) for t in sums]
        accs = []
        for j in range(HEADS // 2):
            both = dot(v_all[2 * j * head:2 * (j + 1) * head, :], probs[:, 2 * j * tile:2 * (j + 1) * tile])
            accs.append(both[:head, :tile])
            accs.append(both[head:, tile:])
        return tops, sums, accs

    def acc_copy(slot, peer):
        return pltpu.make_async_remote_copy(
            src_ref=acc_out.at[peer], dst_ref=acc_in.at[slot],
            send_sem=acc_send.at[peer], recv_sem=acc_recv.at[slot],
            device_id=(d, peer), device_id_type=MESH)

    def stat_copy(slot, peer):
        return pltpu.make_async_remote_copy(
            src_ref=stat_out.at[peer], dst_ref=stat_in.at[slot],
            send_sem=stat_send.at[peer], recv_sem=stat_recv.at[slot],
            device_id=(d, peer), device_id_type=MESH)

    for off in src_order:
        r = src_peer(off)
        q_copy(r, r).wait_recv()
        tops, sums, accs = attend(r)
        stat_out[r] = jnp.concatenate(tops + sums, axis=0)
        acc_out[r] = jnp.concatenate(accs, axis=0).astype(jnp.bfloat16)
        acc_copy(s, r).start()
        stat_copy(s, r).start()

    tops, sums, accs = attend(s)
    parts = [(tops, sums, accs)]
    for off in src_order:
        c = src_peer(off)
        acc_copy(c, c).wait_recv()
        stat_copy(c, c).wait_recv()
        stat = stat_in[c]
        acc = acc_in[c].astype(jnp.float32)
        parts.append((
            [stat[h:h + 1] for h in range(HEADS)],
            [stat[HEADS + h:HEADS + h + 1] for h in range(HEADS)],
            [acc[h * head:(h + 1) * head] for h in range(HEADS)],
        ))

    mixed = []
    for h in range(HEADS):
        top = self_score[h]
        for tops, _, _ in parts:
            top = jnp.maximum(top, tops[h])
        weight = jnp.exp(self_score[h] - top)
        total = weight
        number = weight.astype(jnp.bfloat16).astype(jnp.float32) * own_v[h * head:(h + 1) * head]
        for tops, sums, accs in parts:
            factor = jnp.exp(tops[h] - top)
            total = total + sums[h] * factor
            number = number + accs[h] * factor
        mixed.append(number / total)
    mixed = jnp.concatenate(mixed, axis=0).T.astype(jnp.bfloat16)
    shifted = tangent.astype(jnp.float32) + dot(mixed, wo_ref[...])
    square = jnp.mean(shifted * shifted, axis=-1, keepdims=True)
    normed = shifted * (1.0 / jnp.sqrt(square + 1e-06)) * gain_ref[...]
    radius = jnp.sqrt(jnp.sum(normed * normed, axis=-1, keepdims=True) + 1e-06)
    out_ref[...] = (normed * sinh_over(radius * (1.0 / math.sqrt(width)))).astype(jnp.bfloat16)

    for off in range(1, n_dst):
        k_copy(d, dst_peer(off)).wait_send()
    for off in src_order:
        r = src_peer(off)
        q_copy(s, r).wait_send()
        acc_copy(s, r).wait_send()
        stat_copy(s, r).wait_send()


def per_device(n_dst, n_src, points, w_query, w_key, w_value, w_out, gain, cell_counts, tile_slots, edge_masks):
    tile = points.shape[0]
    width = points.shape[1]
    n_slots = tile_slots.shape[-1]
    vmem = pl.BlockSpec(memory_space=pltpu.VMEM)
    smem = pl.BlockSpec(memory_space=pltpu.SMEM)
    dma = pltpu.SemaphoreType.DMA
    return pl.pallas_call(
        functools.partial(kernel, n_dst, n_src, tile, n_slots),
        out_shape=jax.ShapeDtypeStruct((tile, width), jnp.bfloat16),
        in_specs=[vmem] * 6 + [smem, smem, pl.BlockSpec(memory_space=pl.ANY)],
        out_specs=vmem,
        scratch_shapes=[
            pltpu.VMEM((n_dst, tile, width), jnp.bfloat16),
            pltpu.VMEM((n_src, tile, width), jnp.bfloat16),
            pltpu.VMEM((n_slots, tile, tile), jnp.int32),
            pltpu.VMEM((n_slots + 1, tile, tile), jnp.float32),
            pltpu.SMEM((n_src * n_dst,), jnp.int32),
            pltpu.VMEM((n_dst * tile, width), jnp.bfloat16),
            pltpu.VMEM((width, n_dst * tile), jnp.bfloat16),
            pltpu.VMEM((n_dst * tile, HEADS * tile), jnp.float32),
            pltpu.VMEM((n_dst * tile, HEADS * tile), jnp.bfloat16),
            pltpu.VMEM((n_src, width, tile), jnp.bfloat16),
            pltpu.VMEM((n_src, 2 * HEADS, tile), jnp.float32),
            pltpu.VMEM((n_src, width, tile), jnp.bfloat16),
            pltpu.VMEM((n_src, 2 * HEADS, tile), jnp.float32),
            dma,
            dma((n_dst,)), dma((n_dst,)),
            dma((n_src,)), dma((n_src,)),
            dma((n_src,)), dma((n_src,)),
            dma((n_src,)), dma((n_src,)),
        ],
        compiler_params=pltpu.CompilerParams(
            collective_id=0, has_side_effects=True, vmem_limit_bytes=44 * 1024 * 1024),
    )(
        points, w_query, w_key, w_value, w_out, gain.reshape(1, width),
        cell_counts.reshape(1), tile_slots.reshape(n_slots), edge_masks.reshape(n_slots, tile, tile),
    )


def solution(mesh):
    return jax.shard_map(
        functools.partial(per_device, mesh.shape["dst"], mesh.shape["src"]),
        mesh=mesh,
        in_specs=(
            P(("dst", "src"), None),
            P(),
            P(),
            P(),
            P(),
            P(),
            P("dst", "src"),
            P("dst", "src", None),
            P("dst", "src", None, None, None),
        ),
        out_specs=P(("dst", "src"), None),
        check_vma=False,
    )
```

```python
import functools
import math

import jax
import jax.numpy as jnp
from jax import lax
from jax.experimental import pallas as pl
from jax.experimental.pallas import tpu as pltpu
from jax.sharding import PartitionSpec as P

HEADS = 4
NEG = -1e30
MESH = pl.DeviceIdType.MESH


def dot(a, b, dims=((1,), (0,))):
    return lax.dot_general(a, b, (dims, ((), ())), preferred_element_type=jnp.float32)


def log_map(points):
    values_f = points.astype(jnp.float32)
    radius = jnp.sqrt(jnp.sum(values_f * values_f, axis=-1, keepdims=True) + 1e-06)
    root_width = math.sqrt(points.shape[-1])
    ratio = radius / root_width
    arc = jnp.log(ratio + jnp.sqrt(ratio * ratio + 1.0))
    return (values_f * (root_width * arc / radius)).astype(jnp.bfloat16)


def sinh_over(x):
    sq = x * x
    series = 1.0 + sq / 6.0 * (1.0 + sq / 20.0 * (1.0 + sq / 42.0 * (1.0 + sq / 72.0)))
    grown = jnp.exp(x)
    return jnp.where(x < 1.0, series, 0.5 * (grown - 1.0 / grown) / x)


def fold_rows(x):
    return x.reshape(x.shape[0] // 8, 8, x.shape[1])


def kernel(
    n_dst, n_src, tile, n_slots,
    points_hbm, wq_hbm, wk_hbm, wv_hbm, wo_hbm, gain_hbm, counts_hbm, slots_hbm, masks_hbm,
    out_ref,
    points_ref, wq_ref, wk_ref, wv_ref, wo_ref, gain_ref, counts_ref, slots_ref, masks,
    kt, qt, bias, inv, wv_turned, q_heads, k_all, v_all, scores, probs, acc_out, stat_out, acc_in, stat_in,
    load_sem, kt_send, kt_recv, qt_send, qt_recv, acc_send, acc_recv, stat_send, stat_recv,
):
    d = lax.axis_index("dst")
    s = lax.axis_index("src")
    width = points_hbm.shape[1]
    head = width // HEADS
    scale = 1.0 / math.sqrt(head)

    def dst_peer(off):
        return lax.rem(d + off, n_dst)

    def src_peer(off):
        return lax.rem(s + off, n_src)

    barrier = pltpu.get_barrier_semaphore()
    for off in range(1, n_src):
        pl.semaphore_signal(barrier, inc=1, device_id=(d, src_peer(off)), device_id_type=MESH)
    for off in range(1, n_dst):
        pl.semaphore_signal(barrier, inc=1, device_id=(dst_peer(off), s), device_id_type=MESH)

    loads = [
        pltpu.make_async_copy(source, target, load_sem.at[index])
        for index, (source, target) in enumerate([
            (points_hbm, points_ref), (slots_hbm, slots_ref), (counts_hbm, counts_ref),
            (wv_hbm, wv_ref), (wk_hbm, wk_ref), (wq_hbm, wq_ref), (masks_hbm, masks),
            (wo_hbm, wo_ref), (gain_hbm, gain_ref),
        ])
    ]
    for load in loads:
        load.start()
    loads[0].wait()
    tangent = log_map(points_ref[...])
    kt[d] = tangent
    qt[s] = tangent
    pl.semaphore_wait(barrier, n_src - 1 + n_dst - 1)

    def q_copy(slot, peer):
        return pltpu.make_async_remote_copy(
            src_ref=qt.at[slot], dst_ref=qt.at[slot],
            send_sem=qt_send.at[peer], recv_sem=qt_recv.at[slot],
            device_id=(d, peer), device_id_type=MESH)

    def k_copy(slot, peer):
        return pltpu.make_async_remote_copy(
            src_ref=kt.at[slot], dst_ref=kt.at[slot],
            send_sem=kt_send.at[peer], recv_sem=kt_recv.at[slot],
            device_id=(peer, s), device_id_type=MESH)

    src_order = [2, 1, 3] if n_src == 4 else list(range(1, n_src))
    for off in src_order:
        q_copy(s, src_peer(off)).start()
    for off in range(1, n_dst):
        k_copy(d, dst_peer(off)).start()

    loads[1].wait()
    loads[2].wait()
    count = counts_ref[0, 0]
    listed = [jnp.where(count > t, slots_ref[0, 0, t], -1) for t in range(n_slots)]

    def find_slots(step, carry):
        for member in range(4):
            index = step * 4 + member
            found = jnp.int32(n_slots)
            for t in range(n_slots):
                found = jnp.where(listed[t] == index, jnp.int32(t), found)
            inv[index] = found
        return carry

    lax.fori_loop(0, n_src * n_dst // 4, find_slots, 0)

    def eye(n):
        same = lax.broadcasted_iota(jnp.int32, (n, n), 0) == lax.broadcasted_iota(jnp.int32, (n, n), 1)
        return jnp.where(same, 1.0, 0.0).astype(jnp.bfloat16)

    def turned(x, ident):
        return dot(ident, x, ((1,), (1,)))

    eye_tile = eye(tile)
    q_heads[...] = jnp.zeros(q_heads.shape, jnp.bfloat16)
    loads[3].wait()
    wv_turned[...] = turned(wv_ref[...], eye(width)).astype(jnp.bfloat16)
    loads[4].wait()
    loads[5].wait()

    loads[6].wait()
    bias[n_slots] = jnp.full((tile, tile), NEG, jnp.float32)

    def turn_masks(step, carry):
        for member in range(8):
            t = step * 8 + member
            bias[t] = turned(jnp.where(masks[0, 0, t] == 1, 0.0, NEG).astype(jnp.bfloat16), eye_tile)
        return carry

    lax.fori_loop(0, n_slots // 8, turn_masks, 0)

    def project_slot(slot):
        rows = kt[slot]
        at = pl.ds(pl.multiple_of(slot * tile, tile), tile)
        k_all[at, :] = dot(rows, wk_ref[...]).astype(jnp.bfloat16)
        v_all[:, at] = dot(wv_turned[...], rows, ((1,), (1,))).astype(jnp.bfloat16)

    own_v = dot(wv_turned[...], tangent, ((1,), (1,))).astype(jnp.bfloat16).astype(jnp.float32)
    project_slot(d)

    def take_keys(off, carry):
        slot = dst_peer(off)
        k_copy(slot, slot).wait_recv()
        project_slot(slot)
        return carry

    lax.fori_loop(1, n_dst, take_keys, 0)

    group = min(8, n_dst)

    def over_groups(body, start):
        if n_dst == group:
            return body(0, start)
        return lax.fori_loop(0, n_dst // group, body, start)

    def attend(r):
        q = (dot(qt[r], wq_ref[...]).astype(jnp.bfloat16).astype(jnp.float32) * scale).astype(jnp.bfloat16)
        for h in range(HEADS):
            q_heads[h * tile:(h + 1) * tile, h * head:(h + 1) * head] = q[:, h * head:(h + 1) * head]

        def score_group(g, tops):
            tops = list(tops)
            for member in range(group):
                k = g * group + member
                at = pl.ds(k * tile, tile) if isinstance(k, int) else pl.ds(pl.multiple_of(k * tile, tile), tile)
                prod = dot(k_all[at, :], q_heads[...], ((1,), (1,)))
                term = bias[inv[r * n_dst + k]]
                for h in range(HEADS):
                    part = prod[:, h * tile:(h + 1) * tile] + term
                    scores[at, h * tile:(h + 1) * tile] = part
                    tops[h] = jnp.maximum(tops[h], jnp.max(fold_rows(part), axis=0))
            return tuple(tops)

        tops = over_groups(score_group, tuple(jnp.full((8, tile), NEG, jnp.float32) for _ in range(HEADS)))
        tops = [jnp.max(t, axis=0, keepdims=True) for t in tops]

        def exp_group(g, sums):
            sums = list(sums)
            for member in range(group):
                k = g * group + member
                at = pl.ds(k * tile, tile) if isinstance(k, int) else pl.ds(pl.multiple_of(k * tile, tile), tile)
                for h in range(HEADS):
                    lanes = slice(h * tile, (h + 1) * tile)
                    p = jnp.exp(scores[at, lanes] - tops[h])
                    sums[h] = sums[h] + jnp.sum(fold_rows(p), axis=0)
                    probs[at, lanes] = p.astype(jnp.bfloat16)
            return tuple(sums)

        sums = over_groups(exp_group, tuple(jnp.zeros((8, tile), jnp.float32) for _ in range(HEADS)))
        sums = [jnp.sum(t, axis=0, keepdims=True) for t in sums]
        accs = []
        for j in range(HEADS // 2):
            both = dot(v_all[2 * j * head:2 * (j + 1) * head, :], probs[:, 2 * j * tile:2 * (j + 1) * tile])
            accs.append(both[:head, :tile])
            accs.append(both[head:, tile:])
        return tops, sums, accs

    def acc_copy(slot, peer):
        return pltpu.make_async_remote_copy(
            src_ref=acc_out.at[peer], dst_ref=acc_in.at[slot],
            send_sem=acc_send.at[peer], recv_sem=acc_recv.at[slot],
            device_id=(d, peer), device_id_type=MESH)

    def stat_copy(slot, peer):
        return pltpu.make_async_remote_copy(
            src_ref=stat_out.at[peer], dst_ref=stat_in.at[slot],
            send_sem=stat_send.at[peer], recv_sem=stat_recv.at[slot],
            device_id=(d, peer), device_id_type=MESH)

    for off in src_order:
        r = src_peer(off)
        q_copy(r, r).wait_recv()
        tops, sums, accs = attend(r)
        stat_out[r] = jnp.concatenate(tops + sums, axis=0)
        acc_out[r] = jnp.concatenate(accs, axis=0).astype(jnp.bfloat16)
        acc_copy(s, r).start()
        stat_copy(s, r).start()

    tops, sums, accs = attend(s)
    own_prod = dot(k_all[pl.ds(pl.multiple_of(d * tile, tile), tile), :], q_heads[...], ((1,), (1,)))
    diagonal = lax.broadcasted_iota(jnp.int32, (tile, tile), 0) == lax.broadcasted_iota(jnp.int32, (tile, tile), 1)
    self_score = [
        jnp.sum(jnp.where(diagonal, own_prod[:, h * tile:(h + 1) * tile], 0.0), axis=0, keepdims=True)
        for h in range(HEADS)
    ]
    parts = [(tops, sums, accs)]
    for off in src_order:
        c = src_peer(off)
        acc_copy(c, c).wait_recv()
        stat_copy(c, c).wait_recv()
        stat = stat_in[c]
        acc = acc_in[c].astype(jnp.float32)
        parts.append((
            [stat[h:h + 1] for h in range(HEADS)],
            [stat[HEADS + h:HEADS + h + 1] for h in range(HEADS)],
            [acc[h * head:(h + 1) * head] for h in range(HEADS)],
        ))

    mixed = []
    for h in range(HEADS):
        top = self_score[h]
        for tops, _, _ in parts:
            top = jnp.maximum(top, tops[h])
        weight = jnp.exp(self_score[h] - top)
        total = weight
        number = weight.astype(jnp.bfloat16).astype(jnp.float32) * own_v[h * head:(h + 1) * head]
        for tops, sums, accs in parts:
            factor = jnp.exp(tops[h] - top)
            total = total + sums[h] * factor
            number = number + accs[h] * factor
        mixed.append(number / total)
    mixed = turned(jnp.concatenate(mixed, axis=0).astype(jnp.bfloat16), eye_tile).astype(jnp.bfloat16)
    loads[7].wait()
    loads[8].wait()
    shifted = tangent.astype(jnp.float32) + dot(mixed, wo_ref[...])
    square = jnp.mean(shifted * shifted, axis=-1, keepdims=True)
    normed = shifted * (1.0 / jnp.sqrt(square + 1e-06)) * gain_ref[...]
    radius = jnp.sqrt(jnp.sum(normed * normed, axis=-1, keepdims=True) + 1e-06)
    out_ref[...] = (normed * sinh_over(radius * (1.0 / math.sqrt(width)))).astype(jnp.bfloat16)

    for off in range(1, n_dst):
        k_copy(d, dst_peer(off)).wait_send()
    for off in src_order:
        r = src_peer(off)
        q_copy(s, r).wait_send()
        acc_copy(s, r).wait_send()
        stat_copy(s, r).wait_send()


def per_device(n_dst, n_src, points, w_query, w_key, w_value, w_out, gain, cell_counts, tile_slots, edge_masks):
    tile = points.shape[0]
    width = points.shape[1]
    n_slots = tile_slots.shape[-1]
    vmem = pl.BlockSpec(memory_space=pltpu.VMEM)
    dma = pltpu.SemaphoreType.DMA
    return pl.pallas_call(
        functools.partial(kernel, n_dst, n_src, tile, n_slots),
        out_shape=jax.ShapeDtypeStruct((tile, width), jnp.bfloat16),
        in_specs=[pl.BlockSpec(memory_space=pltpu.HBM)] * 9,
        out_specs=vmem,
        scratch_shapes=[
            pltpu.VMEM((tile, width), jnp.bfloat16),
            *[pltpu.VMEM((width, width), jnp.bfloat16)] * 4,
            pltpu.VMEM((1, width), jnp.float32),
            pltpu.SMEM((1, 1), jnp.int32),
            pltpu.SMEM((1, 1, n_slots), jnp.int32),
            pltpu.VMEM((1, 1, n_slots, tile, tile), jnp.int32),
            pltpu.VMEM((n_dst, tile, width), jnp.bfloat16),
            pltpu.VMEM((n_src, tile, width), jnp.bfloat16),
            pltpu.VMEM((n_slots + 1, tile, tile), jnp.float32),
            pltpu.SMEM((n_src * n_dst,), jnp.int32),
            pltpu.VMEM((width, width), jnp.bfloat16),
            pltpu.VMEM((HEADS * tile, width), jnp.bfloat16),
            pltpu.VMEM((n_dst * tile, width), jnp.bfloat16),
            pltpu.VMEM((width, n_dst * tile), jnp.bfloat16),
            pltpu.VMEM((n_dst * tile, HEADS * tile), jnp.float32),
            pltpu.VMEM((n_dst * tile, HEADS * tile), jnp.bfloat16),
            pltpu.VMEM((n_src, width, tile), jnp.bfloat16),
            pltpu.VMEM((n_src, 2 * HEADS, tile), jnp.float32),
            pltpu.VMEM((n_src, width, tile), jnp.bfloat16),
            pltpu.VMEM((n_src, 2 * HEADS, tile), jnp.float32),
            dma((9,)),
            dma((n_dst,)), dma((n_dst,)),
            dma((n_src,)), dma((n_src,)),
            dma((n_src,)), dma((n_src,)),
            dma((n_src,)), dma((n_src,)),
        ],
        compiler_params=pltpu.CompilerParams(
            collective_id=0, has_side_effects=True, vmem_limit_bytes=58 * 1024 * 1024),
    )(
        points, w_query, w_key, w_value, w_out, gain.reshape(1, width),
        cell_counts, tile_slots, edge_masks,
    )


def solution(mesh):
    return jax.shard_map(
        functools.partial(per_device, mesh.shape["dst"], mesh.shape["src"]),
        mesh=mesh,
        in_specs=(
            P(("dst", "src"), None),
            P(),
            P(),
            P(),
            P(),
            P(),
            P("dst", "src"),
            P("dst", "src", None),
            P("dst", "src", None, None, None),
        ),
        out_specs=P(("dst", "src"), None),
        check_vma=False,
    )
```

```python
import functools
import math

import jax
import jax.numpy as jnp
from jax import lax
from jax.experimental import pallas as pl
from jax.experimental.pallas import tpu as pltpu
from jax.sharding import PartitionSpec as P

HEADS = 4
NEG = -1e30
MESH = pl.DeviceIdType.MESH


def dot(a, b, dims=((1,), (0,))):
    return lax.dot_general(a, b, (dims, ((), ())), preferred_element_type=jnp.float32)


def log_map(points):
    values_f = points.astype(jnp.float32)
    radius = jnp.sqrt(jnp.sum(values_f * values_f, axis=-1, keepdims=True) + 1e-06)
    root_width = math.sqrt(points.shape[-1])
    ratio = radius / root_width
    arc = jnp.log(ratio + jnp.sqrt(ratio * ratio + 1.0))
    return (values_f * (root_width * arc / radius)).astype(jnp.bfloat16)


def sinh_over(x):
    sq = x * x
    series = 1.0 + sq / 6.0 * (1.0 + sq / 20.0 * (1.0 + sq / 42.0 * (1.0 + sq / 72.0)))
    grown = jnp.exp(x)
    return jnp.where(x < 1.0, series, 0.5 * (grown - 1.0 / grown) / x)


def fold_rows(x):
    return x.reshape(x.shape[0] // 8, 8, x.shape[1])


def kernel(
    n_dst, n_src, tile, n_slots,
    points_hbm, wq_hbm, wk_hbm, wv_hbm, wo_hbm, gain_hbm, counts_hbm, slots_hbm, masks_hbm,
    out_ref,
    points_ref, wq_ref, wk_ref, wv_ref, wo_ref, gain_ref, counts_ref, slots_ref, masks,
    kt, qt, bias, inv, wv_turned, q_heads, k_all, v_all, scores, probs, tops, row_tops, sums, acc_out, stat_out, acc_in, stat_in,
    load_sem, kt_send, kt_recv, qt_send, qt_recv, acc_send, acc_recv, stat_send, stat_recv,
):
    d = lax.axis_index("dst")
    s = lax.axis_index("src")
    width = points_hbm.shape[1]
    head = width // HEADS
    scale = 1.0 / math.sqrt(head)

    def dst_peer(off):
        return lax.rem(d + off, n_dst)

    def src_peer(off):
        return lax.rem(s + off, n_src)

    barrier = pltpu.get_barrier_semaphore()
    for off in range(1, n_src):
        pl.semaphore_signal(barrier, inc=1, device_id=(d, src_peer(off)), device_id_type=MESH)
    for off in range(1, n_dst):
        pl.semaphore_signal(barrier, inc=1, device_id=(dst_peer(off), s), device_id_type=MESH)

    loads = [
        pltpu.make_async_copy(source, target, load_sem.at[index])
        for index, (source, target) in enumerate([
            (points_hbm, points_ref), (slots_hbm, slots_ref), (counts_hbm, counts_ref),
            (wv_hbm, wv_ref), (wk_hbm, wk_ref), (wq_hbm, wq_ref), (masks_hbm, masks),
            (wo_hbm, wo_ref), (gain_hbm, gain_ref),
        ])
    ]
    for load in loads:
        load.start()
    loads[0].wait()
    tangent = log_map(points_ref[...])
    kt[d] = tangent
    qt[s] = tangent
    pl.semaphore_wait(barrier, n_src - 1 + n_dst - 1)

    def q_copy(slot, peer):
        return pltpu.make_async_remote_copy(
            src_ref=qt.at[slot], dst_ref=qt.at[slot],
            send_sem=qt_send.at[peer], recv_sem=qt_recv.at[slot],
            device_id=(d, peer), device_id_type=MESH)

    def k_copy(slot, peer):
        return pltpu.make_async_remote_copy(
            src_ref=kt.at[slot], dst_ref=kt.at[slot],
            send_sem=kt_send.at[peer], recv_sem=kt_recv.at[slot],
            device_id=(peer, s), device_id_type=MESH)

    src_order = [2, 1, 3] if n_src == 4 else list(range(1, n_src))
    for off in src_order:
        q_copy(s, src_peer(off)).start()
    for off in range(1, n_dst):
        k_copy(d, dst_peer(off)).start()

    loads[1].wait()
    loads[2].wait()
    count = counts_ref[0, 0]
    listed = [jnp.where(count > t, slots_ref[0, 0, t], -1) for t in range(n_slots)]

    def find_slots(step, carry):
        for member in range(4):
            index = step * 4 + member
            found = jnp.int32(n_slots)
            for t in range(n_slots):
                found = jnp.where(listed[t] == index, jnp.int32(t), found)
            inv[index] = found
        return carry

    lax.fori_loop(0, n_src * n_dst // 4, find_slots, 0)

    def eye(n):
        same = lax.broadcasted_iota(jnp.int32, (n, n), 0) == lax.broadcasted_iota(jnp.int32, (n, n), 1)
        return jnp.where(same, 1.0, 0.0).astype(jnp.bfloat16)

    def turned(x, ident):
        return dot(ident, x, ((1,), (1,)))

    eye_tile = eye(tile)
    q_heads[...] = jnp.zeros(q_heads.shape, jnp.bfloat16)
    loads[3].wait()
    wv_turned[...] = turned(wv_ref[...], eye(width)).astype(jnp.bfloat16)
    loads[4].wait()
    loads[5].wait()

    loads[6].wait()
    tops[:, n_slots] = jnp.full((HEADS // 2, 8, 2 * tile), NEG, jnp.float32)
    sums[:, n_slots] = jnp.zeros((HEADS // 2, 8, 2 * tile), jnp.float32)
    probs[:, n_slots] = jnp.zeros((HEADS // 2, tile, 2 * tile), jnp.bfloat16)

    def turn_masks(step, carry):
        for member in range(8):
            t = step * 8 + member
            bias[t] = turned(jnp.where(masks[0, 0, t] == 1, 0.0, NEG).astype(jnp.bfloat16), eye_tile)
        return carry

    lax.fori_loop(0, n_slots // 8, turn_masks, 0)

    def project_slot(slot):
        rows = kt[slot]
        at = pl.ds(pl.multiple_of(slot * tile, tile), tile)
        k_all[slot] = dot(rows, wk_ref[...]).astype(jnp.bfloat16)
        v_all[:, at] = dot(wv_turned[...], rows, ((1,), (1,))).astype(jnp.bfloat16)

    own_v = dot(wv_turned[...], tangent, ((1,), (1,))).astype(jnp.bfloat16).astype(jnp.float32)
    project_slot(d)

    def take_keys(off, carry):
        slot = dst_peer(off)
        k_copy(slot, slot).wait_recv()
        project_slot(slot)
        return carry

    lax.fori_loop(1, n_dst, take_keys, 0)

    group = min(16, n_slots)
    pairs = HEADS // 2

    def over_slots(body):
        if n_slots == group:
            for t in range(n_slots):
                body(t)
            return

        def some(g, carry):
            for member in range(group):
                body(g * group + member)
            return carry

        lax.fori_loop(0, n_slots // group, some, 0)

    def project_queries(r):
        q = (dot(qt[r], wq_ref[...]).astype(jnp.bfloat16).astype(jnp.float32) * scale).astype(jnp.bfloat16)
        for h in range(HEADS):
            half = h % 2
            q_heads[r, h // 2, half * tile:(half + 1) * tile, half * head:(half + 1) * head] = (
                q[:, h * head:(h + 1) * head])

    def attend(j):
        lanes = slice(2 * j * head, 2 * (j + 1) * head)

        def score(t):
            cell = slots_ref[0, 0, t]
            r = lax.div(cell, jnp.int32(n_dst))
            k = lax.rem(cell, jnp.int32(n_dst))
            prod = dot(k_all[k, :, lanes], q_heads[r, j], ((1,), (1,)))
            term = bias[t]
            for half in range(2):
                at = slice(half * tile, (half + 1) * tile)
                part = prod[:, at] + term
                scores[j, t, :, at] = part
                tops[j, t, :, at] = jnp.max(fold_rows(part), axis=0)

        over_slots(score)
        for r in range(n_src):
            top = tops[j, inv[r * n_dst]]
            for k in range(1, n_dst):
                top = jnp.maximum(top, tops[j, inv[r * n_dst + k]])
            row_tops[j, r] = jnp.broadcast_to(jnp.max(top, axis=0, keepdims=True), top.shape)

        def weigh(t):
            r = lax.div(slots_ref[0, 0, t], jnp.int32(n_dst))
            for half in range(2):
                at = slice(half * tile, (half + 1) * tile)
                p = jnp.exp(fold_rows(scores[j, t, :, at]) - row_tops[j, r, :, at][None])
                sums[j, t, :, at] = jnp.sum(p, axis=0)
                probs[j, t, :, at] = p.reshape(tile, tile).astype(jnp.bfloat16)

        over_slots(weigh)

    def collect(j, r):
        listing = [inv[r * n_dst + k] for k in range(n_dst)]
        total = sums[j, listing[0]]
        for t in listing[1:]:
            total = total + sums[j, t]
        total = jnp.sum(total, axis=0, keepdims=True)
        top = row_tops[j, r][:1]
        both = dot(v_all[2 * j * head:2 * (j + 1) * head, :],
                   jnp.concatenate([probs[j, t] for t in listing], axis=0))
        return (
            [top[:, :tile], top[:, tile:]],
            [total[:, :tile], total[:, tile:]],
            [both[:head, :tile], both[head:, tile:]],
        )

    def acc_copy(j, slot, peer):
        return pltpu.make_async_remote_copy(
            src_ref=acc_out.at[j, peer], dst_ref=acc_in.at[j, slot],
            send_sem=acc_send.at[j, peer], recv_sem=acc_recv.at[j, slot],
            device_id=(d, peer), device_id_type=MESH)

    def stat_copy(j, slot, peer):
        return pltpu.make_async_remote_copy(
            src_ref=stat_out.at[j, peer], dst_ref=stat_in.at[j, slot],
            send_sem=stat_send.at[j, peer], recv_sem=stat_recv.at[j, slot],
            device_id=(d, peer), device_id_type=MESH)

    project_queries(s)
    for off in src_order:
        r = src_peer(off)
        q_copy(r, r).wait_recv()
        project_queries(r)

    own_parts = []
    for j in range(pairs):
        attend(j)
        for off in src_order:
            r = src_peer(off)
            part_tops, part_sums, part_accs = collect(j, r)
            stat_out[j, r] = jnp.concatenate(part_tops + part_sums + part_tops + part_sums, axis=0)
            acc_out[j, r] = jnp.concatenate(part_accs, axis=0).astype(jnp.bfloat16)
            acc_copy(j, s, r).start()
            stat_copy(j, s, r).start()
        own_parts.append(collect(j, s))

    diagonal = lax.broadcasted_iota(jnp.int32, (tile, tile), 0) == lax.broadcasted_iota(jnp.int32, (tile, tile), 1)
    self_score = []
    parts = [tuple(sum((own_parts[j][n] for j in range(pairs)), []) for n in range(3))]
    for j in range(pairs):
        own_prod = dot(k_all[d, :, 2 * j * head:2 * (j + 1) * head], q_heads[s, j], ((1,), (1,)))
        for half in range(2):
            self_score.append(jnp.sum(
                jnp.where(diagonal, own_prod[:, half * tile:(half + 1) * tile], 0.0), axis=0, keepdims=True))
    for off in src_order:
        c = src_peer(off)
        got = ([], [], [])
        for j in range(pairs):
            acc_copy(j, c, c).wait_recv()
            stat_copy(j, c, c).wait_recv()
            stat = stat_in[j, c]
            acc = acc_in[j, c].astype(jnp.float32)
            for half in range(2):
                got[0].append(stat[half:half + 1])
                got[1].append(stat[2 + half:3 + half])
                got[2].append(acc[half * head:(half + 1) * head])
        parts.append(got)

    mixed = []
    for h in range(HEADS):
        top = self_score[h]
        for part in parts:
            top = jnp.maximum(top, part[0][h])
        weight = jnp.exp(self_score[h] - top)
        total = weight
        number = weight.astype(jnp.bfloat16).astype(jnp.float32) * own_v[h * head:(h + 1) * head]
        for part_tops, part_sums, part_accs in parts:
            factor = jnp.exp(part_tops[h] - top)
            total = total + part_sums[h] * factor
            number = number + part_accs[h] * factor
        mixed.append(number / total)
    mixed = turned(jnp.concatenate(mixed, axis=0).astype(jnp.bfloat16), eye_tile).astype(jnp.bfloat16)
    loads[7].wait()
    loads[8].wait()
    shifted = tangent.astype(jnp.float32) + dot(mixed, wo_ref[...])
    square = jnp.mean(shifted * shifted, axis=-1, keepdims=True)
    normed = shifted * (1.0 / jnp.sqrt(square + 1e-06)) * gain_ref[...]
    radius = jnp.sqrt(jnp.sum(normed * normed, axis=-1, keepdims=True) + 1e-06)
    out_ref[...] = (normed * sinh_over(radius * (1.0 / math.sqrt(width)))).astype(jnp.bfloat16)

    for off in range(1, n_dst):
        k_copy(d, dst_peer(off)).wait_send()
    for off in src_order:
        r = src_peer(off)
        q_copy(s, r).wait_send()
        for j in range(pairs):
            acc_copy(j, s, r).wait_send()
            stat_copy(j, s, r).wait_send()


def per_device(n_dst, n_src, points, w_query, w_key, w_value, w_out, gain, cell_counts, tile_slots, edge_masks):
    tile = points.shape[0]
    width = points.shape[1]
    n_slots = tile_slots.shape[-1]
    pairs = HEADS // 2
    vmem = pl.BlockSpec(memory_space=pltpu.VMEM)
    dma = pltpu.SemaphoreType.DMA
    return pl.pallas_call(
        functools.partial(kernel, n_dst, n_src, tile, n_slots),
        out_shape=jax.ShapeDtypeStruct((tile, width), jnp.bfloat16),
        in_specs=[pl.BlockSpec(memory_space=pltpu.HBM)] * 9,
        out_specs=vmem,
        scratch_shapes=[
            pltpu.VMEM((tile, width), jnp.bfloat16),
            *[pltpu.VMEM((width, width), jnp.bfloat16)] * 4,
            pltpu.VMEM((1, width), jnp.float32),
            pltpu.SMEM((1, 1), jnp.int32),
            pltpu.SMEM((1, 1, n_slots), jnp.int32),
            pltpu.VMEM((1, 1, n_slots, tile, tile), jnp.int32),
            pltpu.VMEM((n_dst, tile, width), jnp.bfloat16),
            pltpu.VMEM((n_src, tile, width), jnp.bfloat16),
            pltpu.VMEM((n_slots, tile, tile), jnp.float32),
            pltpu.SMEM((n_src * n_dst,), jnp.int32),
            pltpu.VMEM((width, width), jnp.bfloat16),
            pltpu.VMEM((n_src, pairs, 2 * tile, width // pairs), jnp.bfloat16),
            pltpu.VMEM((n_dst, tile, width), jnp.bfloat16),
            pltpu.VMEM((width, n_dst * tile), jnp.bfloat16),
            pltpu.VMEM((pairs, n_slots, tile, 2 * tile), jnp.float32),
            pltpu.VMEM((pairs, n_slots + 1, tile, 2 * tile), jnp.bfloat16),
            pltpu.VMEM((pairs, n_slots + 1, 8, 2 * tile), jnp.float32),
            pltpu.VMEM((pairs, n_src, 8, 2 * tile), jnp.float32),
            pltpu.VMEM((pairs, n_slots + 1, 8, 2 * tile), jnp.float32),
            pltpu.VMEM((pairs, n_src, width // pairs, tile), jnp.bfloat16),
            pltpu.VMEM((pairs, n_src, 8, tile), jnp.float32),
            pltpu.VMEM((pairs, n_src, width // pairs, tile), jnp.bfloat16),
            pltpu.VMEM((pairs, n_src, 8, tile), jnp.float32),
            dma((9,)),
            dma((n_dst,)), dma((n_dst,)),
            dma((n_src,)), dma((n_src,)),
            dma((pairs, n_src)), dma((pairs, n_src)),
            dma((pairs, n_src)), dma((pairs, n_src)),
        ],
        compiler_params=pltpu.CompilerParams(
            collective_id=0, has_side_effects=True, vmem_limit_bytes=58 * 1024 * 1024),
    )(
        points, w_query, w_key, w_value, w_out, gain.reshape(1, width),
        cell_counts, tile_slots, edge_masks,
    )


def solution(mesh):
    return jax.shard_map(
        functools.partial(per_device, mesh.shape["dst"], mesh.shape["src"]),
        mesh=mesh,
        in_specs=(
            P(("dst", "src"), None),
            P(),
            P(),
            P(),
            P(),
            P(),
            P("dst", "src"),
            P("dst", "src", None),
            P("dst", "src", None, None, None),
        ),
        out_specs=P(("dst", "src"), None),
        check_vma=False,
    )
```

```python
import functools
import math

import jax
import jax.numpy as jnp
from jax import lax
from jax.experimental import pallas as pl
from jax.experimental.pallas import tpu as pltpu
from jax.sharding import PartitionSpec as P

HEADS = 4
NEG = -1e30
MESH = pl.DeviceIdType.MESH


def dot(a, b, dims=((1,), (0,))):
    return lax.dot_general(a, b, (dims, ((), ())), preferred_element_type=jnp.float32)


def log_map(points):
    values_f = points.astype(jnp.float32)
    radius = jnp.sqrt(jnp.sum(values_f * values_f, axis=-1, keepdims=True) + 1e-06)
    root_width = math.sqrt(points.shape[-1])
    ratio = radius / root_width
    arc = jnp.log(ratio + jnp.sqrt(ratio * ratio + 1.0))
    return (values_f * (root_width * arc / radius)).astype(jnp.bfloat16)


def sinh_over(x):
    sq = x * x
    series = 1.0 + sq / 6.0 * (1.0 + sq / 20.0 * (1.0 + sq / 42.0 * (1.0 + sq / 72.0)))
    grown = jnp.exp(x)
    return jnp.where(x < 1.0, series, 0.5 * (grown - 1.0 / grown) / x)


def fold_rows(x):
    return x.reshape(x.shape[0] // 8, 8, x.shape[1])


def kernel(
    n_dst, n_src, tile, n_slots,
    points_hbm, wq_hbm, wk_hbm, wv_hbm, wo_hbm, gain_hbm, counts_hbm, slots_hbm, masks_hbm,
    out_ref,
    points_ref, wq_ref, wk_ref, wv_ref, wo_ref, gain_ref, counts_ref, slots_ref, masks,
    kt, qt, bias, inv, wv_turned, q_heads, k_all, v_all, scores, probs, tops, row_tops, sums, acc_out, stat_out, acc_in, stat_in,
    load_sem, kt_send, kt_pass, kt_recv, qt_send, qt_recv, acc_send, acc_recv, stat_send, stat_recv,
):
    d = lax.axis_index("dst")
    s = lax.axis_index("src")
    width = points_hbm.shape[1]
    head = width // HEADS
    scale = 1.0 / math.sqrt(head)

    def dst_peer(off):
        return lax.rem(d + off, n_dst)

    def src_peer(off):
        return lax.rem(s + off, n_src)

    barrier = pltpu.get_barrier_semaphore()
    for off in range(1, n_src):
        pl.semaphore_signal(barrier, inc=1, device_id=(d, src_peer(off)), device_id_type=MESH)
    twin = d + 1 - 2 * lax.rem(d, 2)
    k_peers = [dst_peer(off) for off in range(2, n_dst, 2)] + [twin]
    for peer in k_peers:
        pl.semaphore_signal(barrier, inc=1, device_id=(peer, s), device_id_type=MESH)

    loads = [
        pltpu.make_async_copy(source, target, load_sem.at[index])
        for index, (source, target) in enumerate([
            (points_hbm, points_ref), (slots_hbm, slots_ref), (counts_hbm, counts_ref),
            (wv_hbm, wv_ref), (wk_hbm, wk_ref), (wq_hbm, wq_ref), (masks_hbm, masks),
            (wo_hbm, wo_ref), (gain_hbm, gain_ref),
        ])
    ]
    for load in loads:
        load.start()
    loads[0].wait()
    tangent = log_map(points_ref[...])
    kt[d] = tangent
    qt[s] = tangent
    pl.semaphore_wait(barrier, n_src - 1 + n_dst // 2)

    def q_copy(slot, peer):
        return pltpu.make_async_remote_copy(
            src_ref=qt.at[slot], dst_ref=qt.at[slot],
            send_sem=qt_send.at[peer], recv_sem=qt_recv.at[slot],
            device_id=(d, peer), device_id_type=MESH)

    def k_copy(slot, peer):
        return pltpu.make_async_remote_copy(
            src_ref=kt.at[slot], dst_ref=kt.at[slot],
            send_sem=kt_send.at[peer], recv_sem=kt_recv.at[slot],
            device_id=(peer, s), device_id_type=MESH)

    def k_pass(slot):
        return pltpu.make_async_remote_copy(
            src_ref=kt.at[slot], dst_ref=kt.at[slot],
            send_sem=kt_pass.at[slot], recv_sem=kt_recv.at[slot],
            device_id=(twin, s), device_id_type=MESH)

    src_order = [2, 1, 3] if n_src == 4 else list(range(1, n_src))
    for off in src_order:
        q_copy(s, src_peer(off)).start()
    for peer in k_peers:
        k_copy(d, peer).start()

    loads[1].wait()
    loads[2].wait()
    count = counts_ref[0, 0]
    listed = [jnp.where(count > t, slots_ref[0, 0, t], -1) for t in range(n_slots)]

    def find_slots(step, carry):
        for member in range(4):
            index = step * 4 + member
            found = jnp.int32(n_slots)
            for t in range(n_slots):
                found = jnp.where(listed[t] == index, jnp.int32(t), found)
            inv[index] = found
        return carry

    lax.fori_loop(0, n_src * n_dst // 4, find_slots, 0)

    def eye(n):
        same = lax.broadcasted_iota(jnp.int32, (n, n), 0) == lax.broadcasted_iota(jnp.int32, (n, n), 1)
        return jnp.where(same, 1.0, 0.0).astype(jnp.bfloat16)

    def turned(x, ident):
        return dot(ident, x, ((1,), (1,)))

    eye_tile = eye(tile)
    q_heads[...] = jnp.zeros(q_heads.shape, jnp.bfloat16)
    loads[3].wait()
    wv_turned[...] = turned(wv_ref[...], eye(width)).astype(jnp.bfloat16)
    loads[4].wait()
    loads[5].wait()

    def project_slot(slot):
        rows = kt[slot]
        at = pl.ds(pl.multiple_of(slot * tile, tile), tile)
        k_all[slot] = dot(rows, wk_ref[...]).astype(jnp.bfloat16)
        v_all[:, at] = dot(wv_turned[...], rows, ((1,), (1,))).astype(jnp.bfloat16)

    own_v = dot(wv_turned[...], tangent, ((1,), (1,))).astype(jnp.bfloat16).astype(jnp.float32)
    project_slot(d)

    k_copy(twin, twin).wait_recv()
    project_slot(twin)

    def pass_keys(half, carry):
        slot = dst_peer(2 * half)
        k_copy(slot, slot).wait_recv()
        k_pass(slot).start()
        project_slot(slot)
        return carry

    lax.fori_loop(1, n_dst // 2, pass_keys, 0)

    loads[6].wait()
    tops[:, n_slots] = jnp.full((HEADS // 2, 8, 2 * tile), NEG, jnp.float32)
    sums[:, n_slots] = jnp.zeros((HEADS // 2, 8, 2 * tile), jnp.float32)
    probs[:, n_slots] = jnp.zeros((HEADS // 2, tile, 2 * tile), jnp.bfloat16)

    def turn_masks(step, carry):
        for member in range(8):
            t = step * 8 + member
            bias[t] = turned(jnp.where(masks[0, 0, t] == 1, 0.0, NEG).astype(jnp.bfloat16), eye_tile)
        return carry

    lax.fori_loop(0, n_slots // 8, turn_masks, 0)

    def take_keys(half, carry):
        slot = lax.rem(twin + 2 * half, n_dst)
        k_copy(slot, slot).wait_recv()
        project_slot(slot)
        return carry

    lax.fori_loop(1, n_dst // 2, take_keys, 0)

    group = min(16, n_slots)
    pairs = HEADS // 2

    def over_slots(body):
        if n_slots == group:
            for t in range(n_slots):
                body(t)
            return

        def some(g, carry):
            for member in range(group):
                body(g * group + member)
            return carry

        lax.fori_loop(0, n_slots // group, some, 0)

    def project_queries(r):
        q = (dot(qt[r], wq_ref[...]).astype(jnp.bfloat16).astype(jnp.float32) * scale).astype(jnp.bfloat16)
        for h in range(HEADS):
            half = h % 2
            q_heads[r, h // 2, half * tile:(half + 1) * tile, half * head:(half + 1) * head] = (
                q[:, h * head:(h + 1) * head])

    def attend(j):
        lanes = slice(2 * j * head, 2 * (j + 1) * head)

        def score(t):
            cell = slots_ref[0, 0, t]
            r = lax.div(cell, jnp.int32(n_dst))
            k = lax.rem(cell, jnp.int32(n_dst))
            prod = dot(k_all[k, :, lanes], q_heads[r, j], ((1,), (1,)))
            term = bias[t]
            for half in range(2):
                at = slice(half * tile, (half + 1) * tile)
                part = prod[:, at] + term
                scores[j, t, :, at] = part
                tops[j, t, :, at] = jnp.max(fold_rows(part), axis=0)

        over_slots(score)
        for r in range(n_src):
            top = tops[j, inv[r * n_dst]]
            for k in range(1, n_dst):
                top = jnp.maximum(top, tops[j, inv[r * n_dst + k]])
            row_tops[j, r] = jnp.broadcast_to(jnp.max(top, axis=0, keepdims=True), top.shape)

        def weigh(t):
            r = lax.div(slots_ref[0, 0, t], jnp.int32(n_dst))
            for half in range(2):
                at = slice(half * tile, (half + 1) * tile)
                p = jnp.exp(fold_rows(scores[j, t, :, at]) - row_tops[j, r, :, at][None])
                sums[j, t, :, at] = jnp.sum(p, axis=0)
                probs[j, t, :, at] = p.reshape(tile, tile).astype(jnp.bfloat16)

        over_slots(weigh)

    def collect(j, r):
        listing = [inv[r * n_dst + k] for k in range(n_dst)]
        total = sums[j, listing[0]]
        for t in listing[1:]:
            total = total + sums[j, t]
        total = jnp.sum(total, axis=0, keepdims=True)
        top = row_tops[j, r][:1]
        both = dot(v_all[2 * j * head:2 * (j + 1) * head, :],
                   jnp.concatenate([probs[j, t] for t in listing], axis=0))
        return (
            [top[:, :tile], top[:, tile:]],
            [total[:, :tile], total[:, tile:]],
            [both[:head, :tile], both[head:, tile:]],
        )

    def acc_copy(j, slot, peer):
        return pltpu.make_async_remote_copy(
            src_ref=acc_out.at[j, peer], dst_ref=acc_in.at[j, slot],
            send_sem=acc_send.at[j, peer], recv_sem=acc_recv.at[j, slot],
            device_id=(d, peer), device_id_type=MESH)

    def stat_copy(j, slot, peer):
        return pltpu.make_async_remote_copy(
            src_ref=stat_out.at[j, peer], dst_ref=stat_in.at[j, slot],
            send_sem=stat_send.at[j, peer], recv_sem=stat_recv.at[j, slot],
            device_id=(d, peer), device_id_type=MESH)

    project_queries(s)
    for off in src_order:
        r = src_peer(off)
        q_copy(r, r).wait_recv()
        project_queries(r)

    own_parts = []
    for j in range(pairs):
        attend(j)
        for off in src_order:
            r = src_peer(off)
            part_tops, part_sums, part_accs = collect(j, r)
            stat_out[j, r] = jnp.concatenate(part_tops + part_sums + part_tops + part_sums, axis=0)
            acc_out[j, r] = jnp.concatenate(part_accs, axis=0).astype(jnp.bfloat16)
            acc_copy(j, s, r).start()
            stat_copy(j, s, r).start()
        own_parts.append(collect(j, s))

    diagonal = lax.broadcasted_iota(jnp.int32, (tile, tile), 0) == lax.broadcasted_iota(jnp.int32, (tile, tile), 1)
    self_score = []
    parts = [tuple(sum((own_parts[j][n] for j in range(pairs)), []) for n in range(3))]
    for j in range(pairs):
        own_prod = dot(k_all[d, :, 2 * j * head:2 * (j + 1) * head], q_heads[s, j], ((1,), (1,)))
        for half in range(2):
            self_score.append(jnp.sum(
                jnp.where(diagonal, own_prod[:, half * tile:(half + 1) * tile], 0.0), axis=0, keepdims=True))
    for off in src_order:
        c = src_peer(off)
        got = ([], [], [])
        for j in range(pairs):
            acc_copy(j, c, c).wait_recv()
            stat_copy(j, c, c).wait_recv()
            stat = stat_in[j, c]
            acc = acc_in[j, c].astype(jnp.float32)
            for half in range(2):
                got[0].append(stat[half:half + 1])
                got[1].append(stat[2 + half:3 + half])
                got[2].append(acc[half * head:(half + 1) * head])
        parts.append(got)

    mixed = []
    for h in range(HEADS):
        top = self_score[h]
        for part in parts:
            top = jnp.maximum(top, part[0][h])
        weight = jnp.exp(self_score[h] - top)
        total = weight
        number = weight.astype(jnp.bfloat16).astype(jnp.float32) * own_v[h * head:(h + 1) * head]
        for part_tops, part_sums, part_accs in parts:
            factor = jnp.exp(part_tops[h] - top)
            total = total + part_sums[h] * factor
            number = number + part_accs[h] * factor
        mixed.append(number / total)
    mixed = turned(jnp.concatenate(mixed, axis=0).astype(jnp.bfloat16), eye_tile).astype(jnp.bfloat16)
    loads[7].wait()
    loads[8].wait()
    shifted = tangent.astype(jnp.float32) + dot(mixed, wo_ref[...])
    square = jnp.mean(shifted * shifted, axis=-1, keepdims=True)
    normed = shifted * (1.0 / jnp.sqrt(square + 1e-06)) * gain_ref[...]
    radius = jnp.sqrt(jnp.sum(normed * normed, axis=-1, keepdims=True) + 1e-06)
    out_ref[...] = (normed * sinh_over(radius * (1.0 / math.sqrt(width)))).astype(jnp.bfloat16)

    for peer in k_peers:
        k_copy(d, peer).wait_send()
    for half in range(1, n_dst // 2):
        k_pass(dst_peer(2 * half)).wait_send()
    for off in src_order:
        r = src_peer(off)
        q_copy(s, r).wait_send()
        for j in range(pairs):
            acc_copy(j, s, r).wait_send()
            stat_copy(j, s, r).wait_send()


def per_device(n_dst, n_src, points, w_query, w_key, w_value, w_out, gain, cell_counts, tile_slots, edge_masks):
    tile = points.shape[0]
    width = points.shape[1]
    n_slots = tile_slots.shape[-1]
    pairs = HEADS // 2
    vmem = pl.BlockSpec(memory_space=pltpu.VMEM)
    dma = pltpu.SemaphoreType.DMA
    return pl.pallas_call(
        functools.partial(kernel, n_dst, n_src, tile, n_slots),
        out_shape=jax.ShapeDtypeStruct((tile, width), jnp.bfloat16),
        in_specs=[pl.BlockSpec(memory_space=pltpu.HBM)] * 9,
        out_specs=vmem,
        scratch_shapes=[
            pltpu.VMEM((tile, width), jnp.bfloat16),
            *[pltpu.VMEM((width, width), jnp.bfloat16)] * 4,
            pltpu.VMEM((1, width), jnp.float32),
            pltpu.SMEM((1, 1), jnp.int32),
            pltpu.SMEM((1, 1, n_slots), jnp.int32),
            pltpu.VMEM((1, 1, n_slots, tile, tile), jnp.int32),
            pltpu.VMEM((n_dst, tile, width), jnp.bfloat16),
            pltpu.VMEM((n_src, tile, width), jnp.bfloat16),
            pltpu.VMEM((n_slots, tile, tile), jnp.float32),
            pltpu.SMEM((n_src * n_dst,), jnp.int32),
            pltpu.VMEM((width, width), jnp.bfloat16),
            pltpu.VMEM((n_src, pairs, 2 * tile, width // pairs), jnp.bfloat16),
            pltpu.VMEM((n_dst, tile, width), jnp.bfloat16),
            pltpu.VMEM((width, n_dst * tile), jnp.bfloat16),
            pltpu.VMEM((pairs, n_slots, tile, 2 * tile), jnp.float32),
            pltpu.VMEM((pairs, n_slots + 1, tile, 2 * tile), jnp.bfloat16),
            pltpu.VMEM((pairs, n_slots + 1, 8, 2 * tile), jnp.float32),
            pltpu.VMEM((pairs, n_src, 8, 2 * tile), jnp.float32),
            pltpu.VMEM((pairs, n_slots + 1, 8, 2 * tile), jnp.float32),
            pltpu.VMEM((pairs, n_src, width // pairs, tile), jnp.bfloat16),
            pltpu.VMEM((pairs, n_src, 8, tile), jnp.float32),
            pltpu.VMEM((pairs, n_src, width // pairs, tile), jnp.bfloat16),
            pltpu.VMEM((pairs, n_src, 8, tile), jnp.float32),
            dma((9,)),
            dma((n_dst,)), dma((n_dst,)), dma((n_dst,)),
            dma((n_src,)), dma((n_src,)),
            dma((pairs, n_src)), dma((pairs, n_src)),
            dma((pairs, n_src)), dma((pairs, n_src)),
        ],
        compiler_params=pltpu.CompilerParams(
            collective_id=0, has_side_effects=True, vmem_limit_bytes=58 * 1024 * 1024),
    )(
        points, w_query, w_key, w_value, w_out, gain.reshape(1, width),
        cell_counts, tile_slots, edge_masks,
    )


def solution(mesh):
    return jax.shard_map(
        functools.partial(per_device, mesh.shape["dst"], mesh.shape["src"]),
        mesh=mesh,
        in_specs=(
            P(("dst", "src"), None),
            P(),
            P(),
            P(),
            P(),
            P(),
            P("dst", "src"),
            P("dst", "src", None),
            P("dst", "src", None, None, None),
        ),
        out_specs=P(("dst", "src"), None),
        check_vma=False,
    )
```

```python
import functools
import math

import jax
import jax.numpy as jnp
from jax import lax
from jax.experimental import pallas as pl
from jax.experimental.pallas import tpu as pltpu
from jax.sharding import PartitionSpec as P

HEADS = 4
NEG = -1e30
MESH = pl.DeviceIdType.MESH


def dot(a, b, dims=((1,), (0,))):
    return lax.dot_general(a, b, (dims, ((), ())), preferred_element_type=jnp.float32)


def log_map(points):
    values_f = points.astype(jnp.float32)
    radius = jnp.sqrt(jnp.sum(values_f * values_f, axis=-1, keepdims=True) + 1e-06)
    root_width = math.sqrt(points.shape[-1])
    ratio = radius / root_width
    arc = jnp.log(ratio + jnp.sqrt(ratio * ratio + 1.0))
    return (values_f * (root_width * arc / radius)).astype(jnp.bfloat16)


def sinh_over(x):
    sq = x * x
    series = 1.0 + sq / 6.0 * (1.0 + sq / 20.0 * (1.0 + sq / 42.0 * (1.0 + sq / 72.0)))
    grown = jnp.exp(x)
    return jnp.where(x < 1.0, series, 0.5 * (grown - 1.0 / grown) / x)


def fold_rows(x):
    return x.reshape(x.shape[0] // 8, 8, x.shape[1])


def kernel(
    n_dst, n_src, tile, n_slots,
    points_hbm, wq_hbm, wk_hbm, wv_hbm, wo_hbm, gain_hbm, counts_hbm, slots_hbm, masks_hbm,
    out_ref,
    points_ref, wq_ref, wk_ref, wv_ref, wo_ref, gain_ref, counts_ref, slots_ref, masks,
    kt, qt, bias, inv, wv_turned, q_heads, k_all, v_all, scores, probs, tops, row_tops, sums, acc_out, stat_out, acc_in, stat_in,
    load_sem, kt_send, kt_pass, kt_recv, qt_send, qt_pass, qt_recv, acc_send, acc_recv, stat_send, stat_recv,
):
    d = lax.axis_index("dst")
    s = lax.axis_index("src")
    width = points_hbm.shape[1]
    head = width // HEADS
    scale = 1.0 / math.sqrt(head)

    def dst_peer(off):
        return lax.rem(d + off, n_dst)

    def src_peer(off):
        return lax.rem(s + off, n_src)

    barrier = pltpu.get_barrier_semaphore()
    for off in range(1, n_src):
        pl.semaphore_signal(barrier, inc=1, device_id=(d, src_peer(off)), device_id_type=MESH)
    twin = d + 1 - 2 * lax.rem(d, 2)
    k_peers = [dst_peer(off) for off in range(2, n_dst, 2)] + [twin]
    for peer in k_peers:
        pl.semaphore_signal(barrier, inc=1, device_id=(peer, s), device_id_type=MESH)

    loads = [
        pltpu.make_async_copy(source, target, load_sem.at[index])
        for index, (source, target) in enumerate([
            (points_hbm, points_ref), (slots_hbm, slots_ref), (counts_hbm, counts_ref),
            (wv_hbm, wv_ref), (wk_hbm, wk_ref), (wq_hbm, wq_ref), (masks_hbm, masks),
            (wo_hbm, wo_ref), (gain_hbm, gain_ref),
        ])
    ]
    for load in loads:
        load.start()
    loads[0].wait()
    tangent = log_map(points_ref[...])
    kt[d] = tangent
    qt[s] = tangent
    pl.semaphore_wait(barrier, n_src - 1 + n_dst // 2)

    def q_copy(slot, peer):
        return pltpu.make_async_remote_copy(
            src_ref=qt.at[slot], dst_ref=qt.at[slot],
            send_sem=qt_send.at[peer], recv_sem=qt_recv.at[slot],
            device_id=(d, peer), device_id_type=MESH)

    def q_pass(slot):
        return pltpu.make_async_remote_copy(
            src_ref=qt.at[slot], dst_ref=qt.at[slot],
            send_sem=qt_pass.at[0], recv_sem=qt_recv.at[slot],
            device_id=(d, n_src - 1 - slot), device_id_type=MESH)

    def k_copy(slot, peer):
        return pltpu.make_async_remote_copy(
            src_ref=kt.at[slot], dst_ref=kt.at[slot],
            send_sem=kt_send.at[peer], recv_sem=kt_recv.at[slot],
            device_id=(peer, s), device_id_type=MESH)

    def k_pass(slot):
        return pltpu.make_async_remote_copy(
            src_ref=kt.at[slot], dst_ref=kt.at[slot],
            send_sem=kt_pass.at[slot], recv_sem=kt_recv.at[slot],
            device_id=(twin, s), device_id_type=MESH)

    src_order = [2, 1, 3] if n_src == 4 else list(range(1, n_src))
    relayed = n_src == 4
    at_end = jnp.logical_or(s == 0, s == n_src - 1)

    def if_direct(peer, body):
        if relayed:
            pl.when(jnp.logical_not(jnp.logical_and(at_end, peer + s == n_src - 1)))(body)
        else:
            body()

    for off in src_order:
        if_direct(src_peer(off), lambda: q_copy(s, src_peer(off)).start())
    for peer in k_peers:
        k_copy(d, peer).start()

    loads[1].wait()
    loads[2].wait()
    count = counts_ref[0, 0]
    listed = [jnp.where(count > t, slots_ref[0, 0, t], -1) for t in range(n_slots)]

    def find_slots(step, carry):
        for member in range(4):
            index = step * 4 + member
            found = jnp.int32(n_slots)
            for t in range(n_slots):
                found = jnp.where(listed[t] == index, jnp.int32(t), found)
            inv[index] = found
        return carry

    lax.fori_loop(0, n_src * n_dst // 4, find_slots, 0)

    def eye(n):
        same = lax.broadcasted_iota(jnp.int32, (n, n), 0) == lax.broadcasted_iota(jnp.int32, (n, n), 1)
        return jnp.where(same, 1.0, 0.0).astype(jnp.bfloat16)

    def turned(x, ident):
        return dot(ident, x, ((1,), (1,)))

    eye_tile = eye(tile)
    q_heads[...] = jnp.zeros(q_heads.shape, jnp.bfloat16)
    loads[3].wait()
    wv_turned[...] = turned(wv_ref[...], eye(width)).astype(jnp.bfloat16)
    loads[4].wait()
    loads[5].wait()

    def project_slot(slot):
        rows = kt[slot]
        at = pl.ds(pl.multiple_of(slot * tile, tile), tile)
        k_all[slot] = dot(rows, wk_ref[...]).astype(jnp.bfloat16)
        v_all[:, at] = dot(wv_turned[...], rows, ((1,), (1,))).astype(jnp.bfloat16)

    own_v = dot(wv_turned[...], tangent, ((1,), (1,))).astype(jnp.bfloat16).astype(jnp.float32)
    project_slot(d)

    k_copy(twin, twin).wait_recv()
    project_slot(twin)

    def pass_keys(half, carry):
        slot = dst_peer(2 * half)
        k_copy(slot, slot).wait_recv()
        k_pass(slot).start()
        project_slot(slot)
        return carry

    lax.fori_loop(1, n_dst // 2, pass_keys, 0)

    if relayed:
        across = src_peer(2)
        q_copy(across, across).wait_recv()

        @pl.when(jnp.logical_not(at_end))
        def _():
            q_pass(across).start()

    loads[6].wait()
    tops[:, n_slots] = jnp.full((HEADS // 2, 8, 2 * tile), NEG, jnp.float32)
    sums[:, n_slots] = jnp.zeros((HEADS // 2, 8, 2 * tile), jnp.float32)
    probs[:, n_slots] = jnp.zeros((HEADS // 2, tile, 2 * tile), jnp.bfloat16)

    def turn_masks(step, carry):
        for member in range(8):
            t = step * 8 + member
            bias[t] = turned(jnp.where(masks[0, 0, t] == 1, 0.0, NEG).astype(jnp.bfloat16), eye_tile)
        return carry

    lax.fori_loop(0, n_slots // 8, turn_masks, 0)

    def take_keys(half, carry):
        slot = lax.rem(twin + 2 * half, n_dst)
        k_copy(slot, slot).wait_recv()
        project_slot(slot)
        return carry

    lax.fori_loop(1, n_dst // 2, take_keys, 0)

    group = min(16, n_slots)
    pairs = HEADS // 2

    def over_slots(body):
        if n_slots == group:
            for t in range(n_slots):
                body(t)
            return

        def some(g, carry):
            for member in range(group):
                body(g * group + member)
            return carry

        lax.fori_loop(0, n_slots // group, some, 0)

    def project_queries(r):
        q = (dot(qt[r], wq_ref[...]).astype(jnp.bfloat16).astype(jnp.float32) * scale).astype(jnp.bfloat16)
        for h in range(HEADS):
            half = h % 2
            q_heads[r, h // 2, half * tile:(half + 1) * tile, half * head:(half + 1) * head] = (
                q[:, h * head:(h + 1) * head])

    def attend(j):
        lanes = slice(2 * j * head, 2 * (j + 1) * head)

        def score(t):
            cell = slots_ref[0, 0, t]
            r = lax.div(cell, jnp.int32(n_dst))
            k = lax.rem(cell, jnp.int32(n_dst))
            prod = dot(k_all[k, :, lanes], q_heads[r, j], ((1,), (1,)))
            term = bias[t]
            for half in range(2):
                at = slice(half * tile, (half + 1) * tile)
                part = prod[:, at] + term
                scores[j, t, :, at] = part
                tops[j, t, :, at] = jnp.max(fold_rows(part), axis=0)

        over_slots(score)
        for r in range(n_src):
            top = tops[j, inv[r * n_dst]]
            for k in range(1, n_dst):
                top = jnp.maximum(top, tops[j, inv[r * n_dst + k]])
            row_tops[j, r] = jnp.broadcast_to(jnp.max(top, axis=0, keepdims=True), top.shape)

        def weigh(t):
            r = lax.div(slots_ref[0, 0, t], jnp.int32(n_dst))
            for half in range(2):
                at = slice(half * tile, (half + 1) * tile)
                p = jnp.exp(fold_rows(scores[j, t, :, at]) - row_tops[j, r, :, at][None])
                sums[j, t, :, at] = jnp.sum(p, axis=0)
                probs[j, t, :, at] = p.reshape(tile, tile).astype(jnp.bfloat16)

        over_slots(weigh)

    def collect(j, r):
        listing = [inv[r * n_dst + k] for k in range(n_dst)]
        total = sums[j, listing[0]]
        for t in listing[1:]:
            total = total + sums[j, t]
        total = jnp.sum(total, axis=0, keepdims=True)
        top = row_tops[j, r][:1]
        both = dot(v_all[2 * j * head:2 * (j + 1) * head, :],
                   jnp.concatenate([probs[j, t] for t in listing], axis=0))
        return (
            [top[:, :tile], top[:, tile:]],
            [total[:, :tile], total[:, tile:]],
            [both[:head, :tile], both[head:, tile:]],
        )

    def acc_copy(j, slot, peer):
        return pltpu.make_async_remote_copy(
            src_ref=acc_out.at[j, peer], dst_ref=acc_in.at[j, slot],
            send_sem=acc_send.at[j, peer], recv_sem=acc_recv.at[j, slot],
            device_id=(d, peer), device_id_type=MESH)

    def stat_copy(j, slot, peer):
        return pltpu.make_async_remote_copy(
            src_ref=stat_out.at[j, peer], dst_ref=stat_in.at[j, slot],
            send_sem=stat_send.at[j, peer], recv_sem=stat_recv.at[j, slot],
            device_id=(d, peer), device_id_type=MESH)

    project_queries(s)
    for off in src_order:
        r = src_peer(off)
        if not (relayed and off == 2):
            q_copy(r, r).wait_recv()
        project_queries(r)

    own_parts = []
    for j in range(pairs):
        attend(j)
        for off in src_order:
            r = src_peer(off)
            part_tops, part_sums, part_accs = collect(j, r)
            stat_out[j, r] = jnp.concatenate(part_tops + part_sums + part_tops + part_sums, axis=0)
            acc_out[j, r] = jnp.concatenate(part_accs, axis=0).astype(jnp.bfloat16)
            acc_copy(j, s, r).start()
            stat_copy(j, s, r).start()
        own_parts.append(collect(j, s))

    diagonal = lax.broadcasted_iota(jnp.int32, (tile, tile), 0) == lax.broadcasted_iota(jnp.int32, (tile, tile), 1)
    self_score = []
    parts = [tuple(sum((own_parts[j][n] for j in range(pairs)), []) for n in range(3))]
    for j in range(pairs):
        own_prod = dot(k_all[d, :, 2 * j * head:2 * (j + 1) * head], q_heads[s, j], ((1,), (1,)))
        for half in range(2):
            self_score.append(jnp.sum(
                jnp.where(diagonal, own_prod[:, half * tile:(half + 1) * tile], 0.0), axis=0, keepdims=True))
    for off in src_order:
        c = src_peer(off)
        got = ([], [], [])
        for j in range(pairs):
            acc_copy(j, c, c).wait_recv()
            stat_copy(j, c, c).wait_recv()
            stat = stat_in[j, c]
            acc = acc_in[j, c].astype(jnp.float32)
            for half in range(2):
                got[0].append(stat[half:half + 1])
                got[1].append(stat[2 + half:3 + half])
                got[2].append(acc[half * head:(half + 1) * head])
        parts.append(got)

    mixed = []
    for h in range(HEADS):
        top = self_score[h]
        for part in parts:
            top = jnp.maximum(top, part[0][h])
        weight = jnp.exp(self_score[h] - top)
        total = weight
        number = weight.astype(jnp.bfloat16).astype(jnp.float32) * own_v[h * head:(h + 1) * head]
        for part_tops, part_sums, part_accs in parts:
            factor = jnp.exp(part_tops[h] - top)
            total = total + part_sums[h] * factor
            number = number + part_accs[h] * factor
        mixed.append(number / total)
    mixed = turned(jnp.concatenate(mixed, axis=0).astype(jnp.bfloat16), eye_tile).astype(jnp.bfloat16)
    loads[7].wait()
    loads[8].wait()
    shifted = tangent.astype(jnp.float32) + dot(mixed, wo_ref[...])
    square = jnp.mean(shifted * shifted, axis=-1, keepdims=True)
    normed = shifted * (1.0 / jnp.sqrt(square + 1e-06)) * gain_ref[...]
    radius = jnp.sqrt(jnp.sum(normed * normed, axis=-1, keepdims=True) + 1e-06)
    out_ref[...] = (normed * sinh_over(radius * (1.0 / math.sqrt(width)))).astype(jnp.bfloat16)

    if relayed:
        @pl.when(jnp.logical_not(at_end))
        def _():
            q_pass(src_peer(2)).wait_send()

    for peer in k_peers:
        k_copy(d, peer).wait_send()
    for half in range(1, n_dst // 2):
        k_pass(dst_peer(2 * half)).wait_send()
    for off in src_order:
        r = src_peer(off)
        if_direct(r, lambda: q_copy(s, r).wait_send())
        for j in range(pairs):
            acc_copy(j, s, r).wait_send()
            stat_copy(j, s, r).wait_send()


def per_device(n_dst, n_src, points, w_query, w_key, w_value, w_out, gain, cell_counts, tile_slots, edge_masks):
    tile = points.shape[0]
    width = points.shape[1]
    n_slots = tile_slots.shape[-1]
    pairs = HEADS // 2
    vmem = pl.BlockSpec(memory_space=pltpu.VMEM)
    dma = pltpu.SemaphoreType.DMA
    return pl.pallas_call(
        functools.partial(kernel, n_dst, n_src, tile, n_slots),
        out_shape=jax.ShapeDtypeStruct((tile, width), jnp.bfloat16),
        in_specs=[pl.BlockSpec(memory_space=pltpu.HBM)] * 9,
        out_specs=vmem,
        scratch_shapes=[
            pltpu.VMEM((tile, width), jnp.bfloat16),
            *[pltpu.VMEM((width, width), jnp.bfloat16)] * 4,
            pltpu.VMEM((1, width), jnp.float32),
            pltpu.SMEM((1, 1), jnp.int32),
            pltpu.SMEM((1, 1, n_slots), jnp.int32),
            pltpu.VMEM((1, 1, n_slots, tile, tile), jnp.int32),
            pltpu.VMEM((n_dst, tile, width), jnp.bfloat16),
            pltpu.VMEM((n_src, tile, width), jnp.bfloat16),
            pltpu.VMEM((n_slots, tile, tile), jnp.float32),
            pltpu.SMEM((n_src * n_dst,), jnp.int32),
            pltpu.VMEM((width, width), jnp.bfloat16),
            pltpu.VMEM((n_src, pairs, 2 * tile, width // pairs), jnp.bfloat16),
            pltpu.VMEM((n_dst, tile, width), jnp.bfloat16),
            pltpu.VMEM((width, n_dst * tile), jnp.bfloat16),
            pltpu.VMEM((pairs, n_slots, tile, 2 * tile), jnp.float32),
            pltpu.VMEM((pairs, n_slots + 1, tile, 2 * tile), jnp.bfloat16),
            pltpu.VMEM((pairs, n_slots + 1, 8, 2 * tile), jnp.float32),
            pltpu.VMEM((pairs, n_src, 8, 2 * tile), jnp.float32),
            pltpu.VMEM((pairs, n_slots + 1, 8, 2 * tile), jnp.float32),
            pltpu.VMEM((pairs, n_src, width // pairs, tile), jnp.bfloat16),
            pltpu.VMEM((pairs, n_src, 8, tile), jnp.float32),
            pltpu.VMEM((pairs, n_src, width // pairs, tile), jnp.bfloat16),
            pltpu.VMEM((pairs, n_src, 8, tile), jnp.float32),
            dma((9,)),
            dma((n_dst,)), dma((n_dst,)), dma((n_dst,)),
            dma((n_src,)), dma((1,)), dma((n_src,)),
            dma((pairs, n_src)), dma((pairs, n_src)),
            dma((pairs, n_src)), dma((pairs, n_src)),
        ],
        compiler_params=pltpu.CompilerParams(
            collective_id=0, has_side_effects=True, vmem_limit_bytes=58 * 1024 * 1024),
    )(
        points, w_query, w_key, w_value, w_out, gain.reshape(1, width),
        cell_counts, tile_slots, edge_masks,
    )


def solution(mesh):
    return jax.shard_map(
        functools.partial(per_device, mesh.shape["dst"], mesh.shape["src"]),
        mesh=mesh,
        in_specs=(
            P(("dst", "src"), None),
            P(),
            P(),
            P(),
            P(),
            P(),
            P("dst", "src"),
            P("dst", "src", None),
            P("dst", "src", None, None, None),
        ),
        out_specs=P(("dst", "src"), None),
        check_vma=False,
    )
```
